512 devices in a mesh: rep: 32 (over z_lo, x), tp: 16 (over y, z_hi, core).
Axes of the slice: x: 4, y: 4, z: 16 (z_hi: 2, z_lo: 8; z = z_hi * 8 + z_lo), core: 2. Of those that a mesh axis runs over, the one named last changes fastest.
Arguments:
- quant_codes: int32 [32, 32, 49152], P('rep', None, 'tp'), may hold values from 0 to 15
- block_scales: float32 [32, 32, 384], P('rep', None, 'tp'), may hold values from 0.02 to 0.2
- outer_params: float32 [32, 49152], P(None, 'tp'), may hold values from -3 to 3
- outer_moment: float32 [32, 49152], P('rep', 'tp'), may hold values from -0.3 to 0.3
- inputs: bfloat16 [8192, 128], P('rep'), may hold values from -6 to 6
- saved_pre: bfloat16 [8192, 49152], P('rep', 'tp'), may hold values from -8 to 8
- grad_out: bfloat16 [8192, 49152], P('rep', 'tp'), may hold values from -0.375 to 0.375
- weights: bfloat16 [32, 128, 49152], P('rep', None, 'tp'), may hold values from -0.5 to 0.5
Outputs:
- new_params: float32 [32, 49152], P(None, 'tp')
- new_moment: float32 [32, 49152], P('rep', 'tp')
- weight_grad: bfloat16 [32, 128, 49152], P('rep', None, 'tp')
- input_grad_t: bfloat16 [128, 8192], P('tp', 'rep')
The draws below stay inside these ranges and needn't reach their ends.
All inputs are finite; a program needn't handle non-finite values.
Results may differ from the reference program's by a relative error of at most 0.0048.
Values sent between devices are 32-bit elements; how exact they have to be, the bound alone decides.
No kernel may reach another device: no remote copies, remote signals or barrier semaphores. Data moves between devices by JAX's collectives and lax.ppermute only.
A program may use at most 64 MiB of HBM per device.

```python
import math
import jax
import jax.numpy as jnp
from jax import lax

FF = 49152
QBLOCK = 128
ROWS = 32
WIN = 128
TOK = 256
TOKENS = 8192
N_REP = 32


def with_ends(entries, own_key, smallest, largest):
    shape = entries.shape
    place = [jax.random.randint(jax.random.fold_in(own_key, axis), (), 0, shape[axis]) for axis in range(len(shape))]
    entries = entries.at[tuple(place)].set(smallest)
    longest = shape.index(max(shape))
    place[longest] = (place[longest] + 1) % shape[longest]
    return entries.at[tuple(place)].set(largest)


def block_levels(stream_key, shape, split, least, high):
    def one(dim, blocks):
        draws = jax.random.uniform(jax.random.fold_in(jax.random.fold_in(stream_key, 6), dim), (blocks,), jnp.float32, least / len(split), high / len(split))
        return jnp.repeat(jnp.exp(draws), shape[dim] // blocks).reshape((-1,) + (1,) * (len(shape) - dim - 1))

    level = one(*split[0])
    for cut in split[1:]:
        level = level * one(*cut)
    return level


def normal_values(stream_key, shape, width, reach, shards=(), held_as=jnp.bfloat16):
    drawn = jax.random.normal(stream_key, shape, jnp.float32) * width
    if len(shards) > 0:
        drawn = block_levels(stream_key, shape, shards, -0.22, 0.18) * drawn
    return jnp.clip(drawn, min=-reach, max=reach).astype(held_as)


def setup_inputs(seed: int = 0) -> dict:
    keys = jax.random.split(jax.random.key(seed), 9)
    quant_codes = with_ends(jax.random.randint(keys[0], (N_REP, ROWS, FF), 0, 16), jax.random.fold_in(keys[0], 1), 0, 15).astype(jnp.int32)
    block_scales = jnp.clip(jnp.exp(math.log(0.2) - 2.3025851 * jax.random.uniform(keys[1], (N_REP, ROWS, FF // QBLOCK), jnp.float32) ** block_levels(keys[1], (N_REP, ROWS, FF // QBLOCK), ((0, 32), (2, 16)), -0.2, 0.2)), 0.02, 0.2)
    outer_params = normal_values(keys[2], (ROWS, FF), 0.5, 3.0, ((1, 16),), jnp.float32)
    outer_moment = normal_values(keys[3], (ROWS, FF), 0.05, 0.3, ((0, 32), (1, 16)), jnp.float32)
    inputs = normal_values(keys[4], (TOKENS, WIN), 1.0, 6.0, ((0, 32),))
    saved_pre = normal_values(keys[5], (TOKENS, FF), 1.5, 8.0, ((0, 32), (1, 16)))
    grad_out = normal_values(keys[6], (TOKENS, FF), TOK ** -0.5, 0.375, ((0, 32), (1, 16)))
    weights = normal_values(keys[7], (N_REP, WIN, FF), 0.08, 0.5, ((0, 32), (2, 16)))
    return {"quant_codes": quant_codes, "block_scales": block_scales, "outer_params": outer_params, "outer_moment": outer_moment, "inputs": inputs, "saved_pre": saved_pre, "grad_out": grad_out, "weights": weights}


outer_rate = 0.7
outer_momentum = 0.9
slope_scale = 0.7978845608028654


def gelu_slope(values):
    cubed_values = values * values * values
    tanh_term = jnp.tanh(slope_scale * (values + 0.044715 * cubed_values))
    return 0.5 * (1.0 + tanh_term) + 0.5 * values * (1.0 - tanh_term * tanh_term) * slope_scale * (1.0 + 0.134145 * values * values)


def reference(quant_codes, block_scales, outer_params, outer_moment, inputs, saved_pre, grad_out, weights):
    centred = quant_codes.astype(jnp.float32) - 7.5
    blocked = centred.reshape(N_REP, ROWS, FF // QBLOCK, QBLOCK) * block_scales[:, :, :, None]
    average = jnp.sum(blocked, axis=0).reshape(ROWS, FF) / N_REP
    new_moment = outer_momentum * outer_moment + average
    new_params = outer_params - outer_rate * (average + outer_momentum * new_moment)

    def one_group(items):
        rows_in, grads, pre_vals, sheet = items
        pre_grad = (grads.astype(jnp.float32) * gelu_slope(pre_vals.astype(jnp.float32))).astype(jnp.bfloat16)
        group_wgrad = jnp.dot(rows_in.T, pre_grad, preferred_element_type=jnp.float32).astype(jnp.bfloat16)
        group_igrad = jnp.dot(sheet, pre_grad.T, preferred_element_type=jnp.float32).astype(jnp.bfloat16)
        return group_wgrad, group_igrad

    weight_grad, pieces = lax.map(one_group, (inputs.reshape(N_REP, TOK, WIN), grad_out.reshape(N_REP, TOK, FF), saved_pre.reshape(N_REP, TOK, FF), weights))
    input_grad_t = jnp.transpose(pieces, (1, 0, 2)).reshape(WIN, N_REP * TOK)
    return (new_params, new_moment, weight_grad, input_grad_t)
```

```python
import functools

import jax
import jax.numpy as jnp
from jax import lax
from jax.experimental import pallas as pl
from jax.experimental.pallas import tpu as pltpu
from jax.sharding import PartitionSpec as P

outer_rate = 0.7
outer_momentum = 0.9
slope_scale = 0.7978845608028654
carry = outer_momentum * outer_momentum / (1.0 + outer_momentum)
param_step = outer_rate * (1.0 + outer_momentum)
moment_rest = outer_momentum - carry
near = 8
block = 128


def full(shape):
    return pl.BlockSpec(shape, lambda *_: (0,) * len(shape))


def dequant_kernel(codes_ref, scales_ref, moment_ref, out_ref, *, groups):
    parts, rows, width = out_ref.shape
    own = lax.broadcasted_iota(jnp.int32, (rows, block), 0) == lax.axis_index("rep")
    for j in range(parts * width // block):
        cols = slice(j * block, (j + 1) * block)
        grads = (codes_ref[0, :, cols].astype(jnp.float32) - 7.5) * (
            scales_ref[0, :, j : j + 1] * (1.0 / groups)
        )
        kept = jnp.where(own, carry * moment_ref[:, cols], 0.0)
        part, at = divmod(j * block, width)
        out_ref[part, :, at : at + block] = grads + kept


def backward_kernel(
    inputs_ref, pre_ref, grad_ref, weights_ref, wgrad_ref, keep_ref, send_ref, total
):
    step = pl.program_id(0)

    @pl.when(step == 0)
    def _():
        total[...] = jnp.zeros_like(total)

    v = pre_ref[...].astype(jnp.float32)
    u = v * v
    t = jnp.tanh(v * (slope_scale + (slope_scale * 0.044715) * u))
    slope = (0.5 + 0.5 * t) * (
        1.0 + (v * (slope_scale + (slope_scale * 0.134145) * u)) * (1.0 - t)
    )
    pre_grad = (grad_ref[...].astype(jnp.float32) * slope).astype(jnp.bfloat16)
    wgrad_ref[0] = lax.dot_general(
        inputs_ref[...], pre_grad, (((0,), (0,)), ((), ())), preferred_element_type=jnp.float32
    ).astype(jnp.bfloat16)
    total[...] += lax.dot_general(
        weights_ref[0], pre_grad, (((1,), (1,)), ((), ())), preferred_element_type=jnp.float32
    ).reshape(total.shape)

    @pl.when(step == pl.num_programs(0) - 1)
    def _():
        core = lax.axis_index("tp") % 2
        for j in range(keep_ref.shape[0]):
            keep_ref[j] = total[2 * j + core]
            send_ref[j] = total[2 * j + 1 - core]


def halve_kernel(kept_ref, came_ref, keep_ref, send_ref, *, bit):
    half = keep_ref.shape[0]
    side = (lax.axis_index("tp") // bit) % 2
    for out_ref, at in ((keep_ref, side * half), (send_ref, (1 - side) * half)):
        out_ref[...] = kept_ref[pl.ds(at, half)] + came_ref[pl.ds(at, half)]


def join_kernel(kept_ref, came_ref, out_ref):
    out_ref[...] = (kept_ref[0] + came_ref[0]).astype(out_ref.dtype)


def outer_kernel(sums_ref, params_ref, moment_ref, params_out_ref, moment_out_ref):
    parts, _, width = sums_ref.shape
    own = lax.axis_index("rep")
    for part in range(parts):
        cols = slice(part * width, (part + 1) * width)
        params_out_ref[:, cols] = params_ref[:, cols] - param_step * sums_ref[part]
        moment_out_ref[:, cols] = (
            sums_ref[part, pl.ds(own, 1), :] + moment_rest * moment_ref[:, cols]
        )


def swap(array, axis, bit):
    size = lax.axis_size(axis)
    return lax.ppermute(array, axis, [(i, i ^ bit) for i in range(size)])


def halve(kept, came, bit):
    half = kept.shape[0] // 2
    part = jax.ShapeDtypeStruct((half,) + kept.shape[1:], jnp.float32)
    return pl.pallas_call(
        functools.partial(halve_kernel, bit=bit), out_shape=(part, part), name=f"halve{bit}"
    )(kept, came)


def on_device(
    quant_codes, block_scales, outer_params, outer_moment, inputs, saved_pre, grad_out, weights
):
    groups = lax.axis_size("rep")
    _, rows, hidden = quant_codes.shape
    tokens, window = inputs.shape
    width = hidden // near
    near_groups = [list(range(i, i + near)) for i in range(0, groups, near)]

    parts = pl.pallas_call(
        functools.partial(dequant_kernel, groups=groups),
        out_shape=jax.ShapeDtypeStruct((near, rows, width), jnp.float32),
        name="dequant",
    )(quant_codes, block_scales, outer_moment)
    parts = lax.all_to_all(parts, "rep", 0, 0, axis_index_groups=near_groups, tiled=True)
    chunk = jnp.sum(parts, axis=0)

    tile = 512
    shares = lax.axis_size("tp")
    half = jax.ShapeDtypeStruct((shares // 2, window // shares, tokens), jnp.float32)
    weight_grad, keep, send = pl.pallas_call(
        backward_kernel,
        grid=(hidden // tile,),
        in_specs=[
            full((tokens, window)),
            pl.BlockSpec((tokens, tile), lambda i: (0, i)),
            pl.BlockSpec((tokens, tile), lambda i: (0, i)),
            pl.BlockSpec((1, window, tile), lambda i: (0, 0, i)),
        ],
        out_specs=[
            pl.BlockSpec((1, window, tile), lambda i: (0, 0, i)),
            full(half.shape),
            full(half.shape),
        ],
        out_shape=(jax.ShapeDtypeStruct((1, window, hidden), jnp.bfloat16), half, half),
        scratch_shapes=[pltpu.VMEM((shares, window // shares, tokens), jnp.float32)],
        cost_estimate=pl.CostEstimate(
            flops=4 * tokens * window * hidden,
            bytes_accessed=4 * tokens * hidden + 4 * window * hidden,
            transcendentals=tokens * hidden,
        ),
        name="backward",
    )(inputs, saved_pre, grad_out, weights)

    chunk = chunk + swap(chunk, "rep", near)
    came = swap(send, "tp", 1)
    keep, send = halve(keep, came, 8)
    came = swap(send, "tp", 8)
    keep, send = halve(keep, came, 4)
    came = swap(send, "tp", 4)
    keep, send = halve(keep, came, 2)
    came = swap(send, "tp", 2)
    input_grad_t = pl.pallas_call(
        join_kernel,
        out_shape=jax.ShapeDtypeStruct((window // shares, tokens), jnp.bfloat16),
        name="join",
    )(keep, came)
    chunk = chunk + swap(chunk, "rep", 2 * near)

    sums = lax.all_to_all(
        jnp.broadcast_to(chunk, (near,) + chunk.shape),
        "rep",
        0,
        0,
        axis_index_groups=near_groups,
        tiled=True,
    )
    new_params, new_moment = pl.pallas_call(
        outer_kernel,
        out_shape=(
            jax.ShapeDtypeStruct(outer_params.shape, jnp.float32),
            jax.ShapeDtypeStruct(outer_moment.shape, jnp.float32),
        ),
        name="outer_step",
    )(sums, outer_params, outer_moment)
    return (new_params, new_moment, weight_grad, input_grad_t)


def solution(mesh):
    in_specs = (
        P("rep", None, "tp"),
        P("rep", None, "tp"),
        P(None, "tp"),
        P("rep", "tp"),
        P("rep", None),
        P("rep", "tp"),
        P("rep", "tp"),
        P("rep", None, "tp"),
    )
    out_specs = (P(None, "tp"), P("rep", "tp"), P("rep", None, "tp"), P("tp", "rep"))
    return jax.shard_map(
        on_device, mesh=mesh, in_specs=in_specs, out_specs=out_specs, check_vma=False
    )
```

```python
import functools

import jax
import jax.numpy as jnp
from jax import lax
from jax.experimental import pallas as pl
from jax.experimental.pallas import tpu as pltpu
from jax.sharding import PartitionSpec as P

outer_rate = 0.7
outer_momentum = 0.9
slope_scale = 0.7978845608028654
carry = outer_momentum * outer_momentum / (1.0 + outer_momentum)
param_step = outer_rate * (1.0 + outer_momentum)
moment_rest = outer_momentum - carry
near = 8
block = 128
small = pltpu.CompilerParams(vmem_limit_bytes=4 << 20)


def full(shape):
    return pl.BlockSpec(shape, lambda *_: (0,) * len(shape))


def dequant_kernel(codes_ref, scales_ref, moment_ref, out_ref, *, groups):
    rows = codes_ref.shape[1]
    per_part = out_ref.shape[1] // rows
    own = lax.broadcasted_iota(jnp.int32, (rows, block), 0) == lax.axis_index("rep")
    scales = scales_ref[0].T * (1.0 / groups)
    for j in range(codes_ref.shape[2] // block):
        cols = slice(j * block, (j + 1) * block)
        grads = (codes_ref[0, :, cols].astype(jnp.float32) - 7.5) * scales[:, j : j + 1]
        kept = jnp.where(own, carry * moment_ref[:, cols], 0.0)
        part, k = divmod(j, per_part)
        out_ref[part, k * rows : (k + 1) * rows] = grads + kept


def backward_kernel(
    inputs_ref, pre_ref, grad_ref, weights_ref, wgrad_ref, send_ref, total
):
    step = pl.program_id(0)

    @pl.when(step == 0)
    def _():
        total[...] = jnp.zeros_like(total)

    v = pre_ref[...].astype(jnp.float32)
    u = v * v
    t = jnp.tanh(v * (slope_scale + (slope_scale * 0.044715) * u))
    slope = (0.5 + 0.5 * t) * (
        1.0 + (v * (slope_scale + (slope_scale * 0.134145) * u)) * (1.0 - t)
    )
    pre_grad = (grad_ref[...].astype(jnp.float32) * slope).astype(jnp.bfloat16)
    wgrad_ref[0] = lax.dot_general(
        inputs_ref[...], pre_grad, (((0,), (0,)), ((), ())), preferred_element_type=jnp.float32
    ).astype(jnp.bfloat16)
    total[...] += lax.dot_general(
        weights_ref[0], pre_grad, (((1,), (1,)), ((), ())), preferred_element_type=jnp.float32
    ).reshape(total.shape)

    @pl.when(step == pl.num_programs(0) - 1)
    def _():
        columns, sides = send_ref.shape[:2]
        for j in range(columns):
            for side in range(sides):
                send_ref[j, side] = total[(j // 2) * 4 + side * 2 + j % 2]


def pack_kernel(chunk_ref, moved_ref, came_ref, keep_ref, out_ref):
    size = chunk_ref.shape[0]
    side = (lax.axis_index("tp") // 2) % 2
    sums = []
    for at in (side, 1 - side):
        piece = came_ref[0, at]
        for j in range(1, came_ref.shape[0]):
            piece += came_ref[j, at]
        sums.append(piece)
    keep_ref[...] = sums[0]
    out_ref[:size] = chunk_ref[...] + moved_ref[...]
    height, width = sums[1].shape
    for k in range(width // block):
        out_ref[size + k * height : size + (k + 1) * height] = sums[1][:, k * block : (k + 1) * block]


def spread_kernel(mine_ref, came_ref, copies_ref, relay_ref):
    size = copies_ref.shape[1]
    copies_ref[...] = jnp.broadcast_to(mine_ref[:size] + came_ref[:size], copies_ref.shape)
    relay_ref[...] = came_ref[size:]


def join_kernel(kept_ref, came_ref, out_ref):
    height, width = out_ref.shape
    for k in range(width // block):
        cols = slice(k * block, (k + 1) * block)
        out_ref[:, cols] = (
            kept_ref[:, cols] + came_ref[k * height : (k + 1) * height]
        ).astype(out_ref.dtype)


def outer_kernel(sums_ref, params_ref, moment_ref, params_out_ref, moment_out_ref):
    rows = params_ref.shape[0]
    per_part = sums_ref.shape[1] // rows
    own = lax.axis_index("rep")
    for j in range(params_ref.shape[1] // block):
        cols = slice(j * block, (j + 1) * block)
        part, k = divmod(j, per_part)
        params_out_ref[:, cols] = (
            params_ref[:, cols] - param_step * sums_ref[part, k * rows : (k + 1) * rows]
        )
        moment_out_ref[:, cols] = (
            sums_ref[part, pl.ds(k * rows + own, 1), :] + moment_rest * moment_ref[:, cols]
        )


def swap(array, axis, bit):
    size = lax.axis_size(axis)
    return lax.ppermute(array, axis, [(i, i ^ bit) for i in range(size)])


def exchange(array, axis, groups):
    return lax.all_to_all(array, axis, 0, 0, axis_index_groups=groups, tiled=True)


def on_device(
    quant_codes, block_scales, outer_params, outer_moment, inputs, saved_pre, grad_out, weights
):
    groups = lax.axis_size("rep")
    _, rows, hidden = quant_codes.shape
    tokens, window = inputs.shape
    size = rows * hidden // (near * block)
    near_groups = [list(range(i, i + near)) for i in range(0, groups, near)]

    parts = pl.pallas_call(
        functools.partial(dequant_kernel, groups=groups),
        out_shape=jax.ShapeDtypeStruct((near, size, block), jnp.float32),
        name="dequant",
    )(quant_codes, jnp.transpose(block_scales, (0, 2, 1)), outer_moment)
    parts, inputs = lax.optimization_barrier((parts, inputs))
    parts = exchange(parts, "rep", near_groups)
    chunk = jnp.sum(parts, axis=0)

    tile = 512
    shares = lax.axis_size("tp")
    piece = (window // shares, tokens)
    sent = jax.ShapeDtypeStruct((shares // 2, 2) + piece, jnp.float32)
    weight_grad, send = pl.pallas_call(
        backward_kernel,
        grid=(hidden // tile,),
        in_specs=[
            full((tokens, window)),
            pl.BlockSpec((tokens, tile), lambda i: (0, i)),
            pl.BlockSpec((tokens, tile), lambda i: (0, i)),
            pl.BlockSpec((1, window, tile), lambda i: (0, 0, i)),
        ],
        out_specs=[
            pl.BlockSpec((1, window, tile), lambda i: (0, 0, i)),
            full(sent.shape),
        ],
        out_shape=(jax.ShapeDtypeStruct((1, window, hidden), jnp.bfloat16), sent),
        scratch_shapes=[pltpu.VMEM((shares,) + piece, jnp.float32)],
        cost_estimate=pl.CostEstimate(
            flops=4 * tokens * window * hidden,
            bytes_accessed=4 * tokens * hidden + 4 * window * hidden,
            transcendentals=tokens * hidden,
        ),
        compiler_params=pltpu.CompilerParams(vmem_limit_bytes=60 << 20),
        name="backward",
    )(inputs, saved_pre, grad_out, weights)

    chunk, send = lax.optimization_barrier((chunk, send))
    column_groups = [
        [i + side + core for i in range(0, shares, 4) for core in (0, 1)] for side in (0, 2)
    ]
    came = exchange(send, "tp", column_groups)
    moved = swap(chunk, "rep", near)
    extra = piece[0] * piece[1] // block
    keep, packed = pl.pallas_call(
        pack_kernel,
        out_shape=(
            jax.ShapeDtypeStruct(piece, jnp.float32),
            jax.ShapeDtypeStruct((size + extra, block), jnp.float32),
        ),
        compiler_params=small,
        name="pack",
    )(chunk, moved, came)
    came = swap(packed, "rep", 2 * near)
    copies, relay = pl.pallas_call(
        spread_kernel,
        out_shape=(
            jax.ShapeDtypeStruct((near, size, block), jnp.float32),
            jax.ShapeDtypeStruct((extra, block), jnp.float32),
        ),
        compiler_params=small,
        name="spread",
    )(packed, came)
    came = lax.ppermute(
        relay,
        ("rep", "tp"),
        [
            (i * shares + j, (i ^ (2 * near)) * shares + (j ^ 2))
            for i in range(groups)
            for j in range(shares)
        ],
    )
    input_grad_t = pl.pallas_call(
        join_kernel,
        out_shape=jax.ShapeDtypeStruct(piece, jnp.bfloat16),
        compiler_params=small,
        name="join",
    )(keep, came)
    sums = exchange(copies, "rep", near_groups)
    new_params, new_moment = pl.pallas_call(
        outer_kernel,
        out_shape=(
            jax.ShapeDtypeStruct(outer_params.shape, jnp.float32),
            jax.ShapeDtypeStruct(outer_moment.shape, jnp.float32),
        ),
        compiler_params=small, name="outer_step",
    )(sums, outer_params, outer_moment)
    return (new_params, new_moment, weight_grad, input_grad_t)


def solution(mesh):
    in_specs = (
        P("rep", None, "tp"),
        P("rep", None, "tp"),
        P(None, "tp"),
        P("rep", "tp"),
        P("rep", None),
        P("rep", "tp"),
        P("rep", "tp"),
        P("rep", None, "tp"),
    )
    out_specs = (P(None, "tp"), P("rep", "tp"), P("rep", None, "tp"), P("tp", "rep"))
    return jax.shard_map(
        on_device, mesh=mesh, in_specs=in_specs, out_specs=out_specs, check_vma=False
    )
```

```python
import functools

import jax
import jax.numpy as jnp
from jax import lax
from jax.experimental import pallas as pl
from jax.experimental.pallas import tpu as pltpu
from jax.sharding import PartitionSpec as P

outer_rate = 0.7
outer_momentum = 0.9
slope_scale = 0.7978845608028654
carry = outer_momentum * outer_momentum / (1.0 + outer_momentum)
param_step = outer_rate * (1.0 + outer_momentum)
moment_rest = outer_momentum - carry
near = 8
block = 128
small = pltpu.CompilerParams(vmem_limit_bytes=4 << 20)


def full(shape):
    return pl.BlockSpec(shape, lambda *_: (0,) * len(shape))


def dequant_kernel(codes_ref, scales_ref, moment_ref, out_ref, *, groups):
    rows = codes_ref.shape[1]
    per_part = out_ref.shape[1] // rows
    own = lax.broadcasted_iota(jnp.int32, (rows, block), 0) == lax.axis_index("rep")
    scales = scales_ref[0].T * (1.0 / groups)
    for j in range(codes_ref.shape[2] // block):
        cols = slice(j * block, (j + 1) * block)
        grads = (codes_ref[0, :, cols].astype(jnp.float32) - 7.5) * scales[:, j : j + 1]
        kept = jnp.where(own, carry * moment_ref[:, cols], 0.0)
        part, k = divmod(j, per_part)
        out_ref[part, k * rows : (k + 1) * rows] = grads + kept


def backward_kernel(
    inputs_ref, pre_ref, grad_ref, weights_ref, wgrad_ref, send_ref, total
):
    step = pl.program_id(0)

    @pl.when(step == 0)
    def _():
        total[...] = jnp.zeros_like(total)

    v = pre_ref[...].astype(jnp.float32)
    u = v * v
    t = jnp.tanh(v * (slope_scale + (slope_scale * 0.044715) * u))
    slope = (0.5 + 0.5 * t) * (
        1.0 + (v * (slope_scale + (slope_scale * 0.134145) * u)) * (1.0 - t)
    )
    pre_grad = (grad_ref[...].astype(jnp.float32) * slope).astype(jnp.bfloat16)
    wgrad_ref[0] = lax.dot_general(
        inputs_ref[...], pre_grad, (((0,), (0,)), ((), ())), preferred_element_type=jnp.float32
    ).astype(jnp.bfloat16)
    total[...] += lax.dot_general(
        weights_ref[0], pre_grad, (((1,), (1,)), ((), ())), preferred_element_type=jnp.float32
    ).reshape(total.shape)

    @pl.when(step == pl.num_programs(0) - 1)
    def _():
        columns, sides = send_ref.shape[:2]
        for j in range(columns):
            for side in range(sides):
                send_ref[j, side] = total[(j // 2) * 4 + side * 2 + j % 2]


def side_kernel(came_ref, keep_ref, send_ref):
    side = (lax.axis_index("tp") // 2) % 2
    for out_ref, at in ((keep_ref, side), (send_ref, 1 - side)):
        piece = came_ref[0, at]
        for j in range(1, came_ref.shape[0]):
            piece += came_ref[j, at]
        out_ref[...] = piece


def add_kernel(mine_ref, came_ref, out_ref):
    out_ref[...] = mine_ref[...] + came_ref[...]


def relay_kernel(came_ref, out_ref):
    out_ref[...] = came_ref[...]


def spread_kernel(mine_ref, came_ref, copies_ref):
    copies_ref[...] = jnp.broadcast_to(mine_ref[...] + came_ref[...], copies_ref.shape)


def finish_kernel(
    sums_ref,
    params_ref,
    moment_ref,
    kept_ref,
    came_ref,
    params_out_ref,
    moment_out_ref,
    igrad_out_ref,
):
    rows = params_ref.shape[0]
    per_part = sums_ref.shape[1] // rows
    own = lax.axis_index("rep")
    for j in range(params_ref.shape[1] // block):
        cols = slice(j * block, (j + 1) * block)
        part, k = divmod(j, per_part)
        params_out_ref[:, cols] = (
            params_ref[:, cols] - param_step * sums_ref[part, k * rows : (k + 1) * rows]
        )
        moment_out_ref[:, cols] = (
            sums_ref[part, pl.ds(k * rows + own, 1), :] + moment_rest * moment_ref[:, cols]
        )
    igrad_out_ref[...] = (kept_ref[...] + came_ref[...]).astype(igrad_out_ref.dtype)


def swap(array, axis, bit):
    size = lax.axis_size(axis)
    return lax.ppermute(array, axis, [(i, i ^ bit) for i in range(size)])


def exchange(array, axis, groups):
    return lax.all_to_all(array, axis, 0, 0, axis_index_groups=groups, tiled=True)


def on_device(
    quant_codes, block_scales, outer_params, outer_moment, inputs, saved_pre, grad_out, weights
):
    groups = lax.axis_size("rep")
    _, rows, hidden = quant_codes.shape
    tokens, window = inputs.shape
    size = rows * hidden // (near * block)
    near_groups = [list(range(i, i + near)) for i in range(0, groups, near)]

    parts = pl.pallas_call(
        functools.partial(dequant_kernel, groups=groups),
        out_shape=jax.ShapeDtypeStruct((near, size, block), jnp.float32),
        name="dequant",
    )(quant_codes, jnp.transpose(block_scales, (0, 2, 1)), outer_moment)
    parts, inputs = lax.optimization_barrier((parts, inputs))
    parts = exchange(parts, "rep", near_groups)
    chunk = jnp.sum(parts, axis=0)

    tile = 512
    shares = lax.axis_size("tp")
    piece = (window // shares, tokens)
    sent = jax.ShapeDtypeStruct((shares // 2, 2) + piece, jnp.float32)
    weight_grad, send = pl.pallas_call(
        backward_kernel,
        grid=(hidden // tile,),
        in_specs=[
            full((tokens, window)),
            pl.BlockSpec((tokens, tile), lambda i: (0, i)),
            pl.BlockSpec((tokens, tile), lambda i: (0, i)),
            pl.BlockSpec((1, window, tile), lambda i: (0, 0, i)),
        ],
        out_specs=[
            pl.BlockSpec((1, window, tile), lambda i: (0, 0, i)),
            full(sent.shape),
        ],
        out_shape=(jax.ShapeDtypeStruct((1, window, hidden), jnp.bfloat16), sent),
        scratch_shapes=[pltpu.VMEM((shares,) + piece, jnp.float32)],
        cost_estimate=pl.CostEstimate(
            flops=4 * tokens * window * hidden,
            bytes_accessed=4 * tokens * hidden + 4 * window * hidden,
            transcendentals=tokens * hidden,
        ),
        compiler_params=pltpu.CompilerParams(vmem_limit_bytes=60 << 20),
        name="backward",
    )(inputs, saved_pre, grad_out, weights)

    chunk, _ = lax.optimization_barrier((chunk, send))
    column_groups = [
        [i + side + core for i in range(0, shares, 4) for core in (0, 1)] for side in (0, 2)
    ]
    came = exchange(send, "tp", column_groups)
    part = jax.ShapeDtypeStruct(piece, jnp.float32)
    keep, send = pl.pallas_call(
        side_kernel, out_shape=(part, part), compiler_params=small, name="column_sum"
    )(came)
    came = lax.ppermute(
        send,
        ("rep", "tp"),
        [
            (i * shares + j, (i ^ (2 * near)) * shares + (j ^ 2))
            for i in range(groups)
            for j in range(shares)
        ],
    )
    moved = swap(chunk, "rep", near)
    chunk = pl.pallas_call(
        add_kernel,
        out_shape=jax.ShapeDtypeStruct(chunk.shape, jnp.float32),
        compiler_params=small,
        cost_estimate=pl.CostEstimate(flops=10**11, bytes_accessed=10**9, transcendentals=0),
        name="pair_sum",
    )(chunk, moved)
    moved = swap(chunk, "rep", 2 * near)
    copies = pl.pallas_call(
        spread_kernel,
        out_shape=jax.ShapeDtypeStruct((near, size, block), jnp.float32),
        compiler_params=small,
        name="spread",
    )(chunk, moved)
    came = pl.pallas_call(
        relay_kernel,
        out_shape=part,
        compiler_params=small,
        cost_estimate=pl.CostEstimate(flops=10**11, bytes_accessed=10**9, transcendentals=0),
        name="relay",
    )(came)
    came = swap(came, "rep", 2 * near)
    sums = exchange(copies, "rep", near_groups)
    new_params, new_moment, input_grad_t = pl.pallas_call(
        finish_kernel,
        out_shape=(
            jax.ShapeDtypeStruct(outer_params.shape, jnp.float32),
            jax.ShapeDtypeStruct(outer_moment.shape, jnp.float32),
            jax.ShapeDtypeStruct(piece, jnp.bfloat16),
        ),
        compiler_params=small,
        name="finish",
    )(sums, outer_params, outer_moment, keep, came)
    return (new_params, new_moment, weight_grad, input_grad_t)


def solution(mesh):
    in_specs = (
        P("rep", None, "tp"),
        P("rep", None, "tp"),
        P(None, "tp"),
        P("rep", "tp"),
        P("rep", None),
        P("rep", "tp"),
        P("rep", "tp"),
        P("rep", None, "tp"),
    )
    out_specs = (P(None, "tp"), P("rep", "tp"), P("rep", None, "tp"), P("tp", "rep"))
    return jax.shard_map(
        on_device, mesh=mesh, in_specs=in_specs, out_specs=out_specs, check_vma=False
    )
```

```python
import functools

import jax
import jax.numpy as jnp
from jax import lax
from jax.experimental import pallas as pl
from jax.experimental.pallas import tpu as pltpu
from jax.sharding import PartitionSpec as P

outer_rate = 0.7
outer_momentum = 0.9
slope_scale = 0.7978845608028654
carry = outer_momentum * outer_momentum / (1.0 + outer_momentum)
param_step = outer_rate * (1.0 + outer_momentum)
moment_rest = outer_momentum - carry
near = 8
block = 128
small = pltpu.CompilerParams(vmem_limit_bytes=4 << 20)


def full(shape):
    return pl.BlockSpec(shape, lambda *_: (0,) * len(shape))


def dequant_kernel(codes_ref, scales_ref, moment_ref, out_ref, *, groups):
    rows = codes_ref.shape[1]
    per_part = out_ref.shape[1] // rows
    own = lax.broadcasted_iota(jnp.int32, (rows, block), 0) == lax.axis_index("rep")
    scales = scales_ref[0].T * (1.0 / groups)
    for j in range(codes_ref.shape[2] // block):
        cols = slice(j * block, (j + 1) * block)
        grads = (codes_ref[0, :, cols].astype(jnp.float32) - 7.5) * scales[:, j : j + 1]
        kept = jnp.where(own, carry * moment_ref[:, cols], 0.0)
        part, k = divmod(j, per_part)
        out_ref[part, k * rows : (k + 1) * rows] = grads + kept


def backward_kernel(
    inputs_ref, pre_ref, grad_ref, weights_ref, wgrad_ref, send_ref, total
):
    step = pl.program_id(0)

    @pl.when(step == 0)
    def _():
        total[...] = jnp.zeros_like(total)

    v = pre_ref[...].astype(jnp.float32)
    u = v * v
    t = jnp.tanh(v * (slope_scale + (slope_scale * 0.044715) * u))
    slope = (0.5 + 0.5 * t) * (
        1.0 + (v * (slope_scale + (slope_scale * 0.134145) * u)) * (1.0 - t)
    )
    pre_grad = (grad_ref[...].astype(jnp.float32) * slope).astype(jnp.bfloat16)
    wgrad_ref[0] = lax.dot_general(
        inputs_ref[...], pre_grad, (((0,), (0,)), ((), ())), preferred_element_type=jnp.float32
    ).astype(jnp.bfloat16)
    total[...] += lax.dot_general(
        weights_ref[0], pre_grad, (((1,), (1,)), ((), ())), preferred_element_type=jnp.float32
    ).reshape(total.shape)

    @pl.when(step == pl.num_programs(0) - 1)
    def _():
        columns, sides = send_ref.shape[:2]
        for j in range(columns):
            for side in range(sides):
                send_ref[j, side] = total[(j // 2) * 4 + side * 2 + j % 2]


def side_kernel(came_ref, keep_ref, send_ref):
    side = (lax.axis_index("tp") // 2) % 2
    for out_ref, at in ((keep_ref, side), (send_ref, 1 - side)):
        piece = came_ref[0, at]
        for j in range(1, came_ref.shape[0]):
            piece += came_ref[j, at]
        out_ref[...] = piece


def add_kernel(mine_ref, came_ref, out_ref):
    out_ref[...] = mine_ref[...] + came_ref[...]


def relay_kernel(came_ref, out_ref):
    out_ref[...] = came_ref[...]


def spread_kernel(mine_ref, came_ref, copies_ref):
    copies_ref[...] = jnp.broadcast_to(mine_ref[...] + came_ref[...], copies_ref.shape)


def finish_kernel(
    sums_ref,
    params_ref,
    moment_ref,
    kept_ref,
    came_ref,
    params_out_ref,
    moment_out_ref,
    igrad_out_ref,
):
    rows = params_ref.shape[0]
    per_part = sums_ref.shape[1] // rows
    own = lax.axis_index("rep")
    for j in range(params_ref.shape[1] // block):
        cols = slice(j * block, (j + 1) * block)
        part, k = divmod(j, per_part)
        params_out_ref[:, cols] = (
            params_ref[:, cols] - param_step * sums_ref[part, k * rows : (k + 1) * rows]
        )
        moment_out_ref[:, cols] = (
            sums_ref[part, pl.ds(k * rows + own, 1), :] + moment_rest * moment_ref[:, cols]
        )
    igrad_out_ref[...] = (kept_ref[...] + came_ref[...]).astype(igrad_out_ref.dtype)


def swap(array, axis, bit):
    size = lax.axis_size(axis)
    return lax.ppermute(array, axis, [(i, i ^ bit) for i in range(size)])


def exchange(array, axis, groups):
    return lax.all_to_all(array, axis, 0, 0, axis_index_groups=groups, tiled=True)


def on_device(
    quant_codes, block_scales, outer_params, outer_moment, inputs, saved_pre, grad_out, weights
):
    groups = lax.axis_size("rep")
    _, rows, hidden = quant_codes.shape
    tokens, window = inputs.shape
    size = rows * hidden // (near * block)
    near_groups = [list(range(i, i + near)) for i in range(0, groups, near)]

    parts = pl.pallas_call(
        functools.partial(dequant_kernel, groups=groups),
        out_shape=jax.ShapeDtypeStruct((near, size, block), jnp.float32),
        name="dequant",
    )(quant_codes, jnp.transpose(block_scales, (0, 2, 1)), outer_moment)
    parts, inputs = lax.optimization_barrier((parts, inputs))
    parts = exchange(parts, "rep", near_groups)
    chunk = jnp.sum(parts, axis=0)

    tile = 1536
    shares = lax.axis_size("tp")
    piece = (window // shares, tokens)
    sent = jax.ShapeDtypeStruct((shares // 2, 2) + piece, jnp.float32)
    weight_grad, send = pl.pallas_call(
        backward_kernel,
        grid=(hidden // tile,),
        in_specs=[
            full((tokens, window)),
            pl.BlockSpec((tokens, tile), lambda i: (0, i)),
            pl.BlockSpec((tokens, tile), lambda i: (0, i)),
            pl.BlockSpec((1, window, tile), lambda i: (0, 0, i)),
        ],
        out_specs=[
            pl.BlockSpec((1, window, tile), lambda i: (0, 0, i)),
            full(sent.shape),
        ],
        out_shape=(jax.ShapeDtypeStruct((1, window, hidden), jnp.bfloat16), sent),
        scratch_shapes=[pltpu.VMEM((shares,) + piece, jnp.float32)],
        cost_estimate=pl.CostEstimate(
            flops=4 * tokens * window * hidden,
            bytes_accessed=4 * tokens * hidden + 4 * window * hidden,
            transcendentals=tokens * hidden,
        ),
        compiler_params=pltpu.CompilerParams(vmem_limit_bytes=60 << 20),
        name="backward",
    )(inputs, saved_pre, grad_out, weights)

    chunk, _ = lax.optimization_barrier((chunk, send))
    column_groups = [
        [i + side + core for i in range(0, shares, 4) for core in (0, 1)] for side in (0, 2)
    ]
    came = exchange(send, "tp", column_groups)
    part = jax.ShapeDtypeStruct(piece, jnp.float32)
    keep, send = pl.pallas_call(
        side_kernel, out_shape=(part, part), compiler_params=small, name="column_sum"
    )(came)
    came = lax.ppermute(
        send,
        ("rep", "tp"),
        [
            (i * shares + j, (i ^ near) * shares + (j ^ 2))
            for i in range(groups)
            for j in range(shares)
        ],
    )
    moved = swap(chunk, "rep", near)
    chunk = pl.pallas_call(
        add_kernel,
        out_shape=jax.ShapeDtypeStruct(chunk.shape, jnp.float32),
        compiler_params=small,
        cost_estimate=pl.CostEstimate(flops=10**11, bytes_accessed=10**9, transcendentals=0),
        name="pair_sum",
    )(chunk, moved)
    moved = swap(chunk, "rep", 2 * near)
    copies = pl.pallas_call(
        spread_kernel,
        out_shape=jax.ShapeDtypeStruct((near, size, block), jnp.float32),
        compiler_params=small,
        name="spread",
    )(chunk, moved)
    came = pl.pallas_call(
        relay_kernel,
        out_shape=part,
        compiler_params=small,
        cost_estimate=pl.CostEstimate(flops=10**11, bytes_accessed=10**9, transcendentals=0),
        name="relay",
    )(came)
    came = swap(came, "rep", near)
    sums = exchange(copies, "rep", near_groups)
    new_params, new_moment, input_grad_t = pl.pallas_call(
        finish_kernel,
        out_shape=(
            jax.ShapeDtypeStruct(outer_params.shape, jnp.float32),
            jax.ShapeDtypeStruct(outer_moment.shape, jnp.float32),
            jax.ShapeDtypeStruct(piece, jnp.bfloat16),
        ),
        compiler_params=small,
        name="finish",
    )(sums, outer_params, outer_moment, keep, came)
    return (new_params, new_moment, weight_grad, input_grad_t)


def solution(mesh):
    in_specs = (
        P("rep", None, "tp"),
        P("rep", None, "tp"),
        P(None, "tp"),
        P("rep", "tp"),
        P("rep", None),
        P("rep", "tp"),
        P("rep", "tp"),
        P("rep", None, "tp"),
    )
    out_specs = (P(None, "tp"), P("rep", "tp"), P("rep", None, "tp"), P("tp", "rep"))
    return jax.shard_map(
        on_device, mesh=mesh, in_specs=in_specs, out_specs=out_specs, check_vma=False
    )
```

```python
import functools

import jax
import jax.numpy as jnp
from jax import lax
from jax.experimental import pallas as pl
from jax.experimental.pallas import tpu as pltpu
from jax.sharding import PartitionSpec as P

outer_rate = 0.7
outer_momentum = 0.9
slope_scale = 0.7978845608028654
carry = outer_momentum * outer_momentum / (1.0 + outer_momentum)
param_step = outer_rate * (1.0 + outer_momentum)
moment_rest = outer_momentum - carry
near = 8
block = 128
small = pltpu.CompilerParams(vmem_limit_bytes=4 << 20)


def full(shape):
    return pl.BlockSpec(shape, lambda *_: (0,) * len(shape))


def dequant_kernel(codes_ref, scales_ref, moment_ref, out_ref, *, groups):
    rows = codes_ref.shape[1]
    per_part = out_ref.shape[1] // rows
    own = lax.broadcasted_iota(jnp.int32, (rows, block), 0) == lax.axis_index("rep")
    scales = scales_ref[0].T * (1.0 / groups)
    for j in range(codes_ref.shape[2] // block):
        cols = slice(j * block, (j + 1) * block)
        grads = (codes_ref[0, :, cols].astype(jnp.float32) - 7.5) * scales[:, j : j + 1]
        kept = jnp.where(own, carry * moment_ref[:, cols], 0.0)
        part, k = divmod(j, per_part)
        out_ref[part, k * rows : (k + 1) * rows] = grads + kept


def backward_kernel(
    inputs_ref, pre_ref, grad_ref, weights_ref, wgrad_ref, send_ref, total
):
    step = pl.program_id(0)

    @pl.when(step == 0)
    def _():
        total[...] = jnp.zeros_like(total)

    v = pre_ref[...].astype(jnp.float32)
    u = v * v
    t = jnp.tanh(v * (slope_scale + (slope_scale * 0.044715) * u))
    slope = (0.5 + 0.5 * t) * (
        1.0 + (v * (slope_scale + (slope_scale * 0.134145) * u)) * (1.0 - t)
    )
    pre_grad = (grad_ref[...].astype(jnp.float32) * slope).astype(jnp.bfloat16)
    wgrad_ref[0] = lax.dot_general(
        inputs_ref[...], pre_grad, (((0,), (0,)), ((), ())), preferred_element_type=jnp.float32
    ).astype(jnp.bfloat16)
    total[...] += lax.dot_general(
        weights_ref[0], pre_grad, (((1,), (1,)), ((), ())), preferred_element_type=jnp.float32
    ).reshape(total.shape)

    @pl.when(step == pl.num_programs(0) - 1)
    def _():
        columns, sides = send_ref.shape[:2]
        for j in range(columns):
            for side in range(sides):
                send_ref[j, side] = total[(j // 2) * 4 + side * 2 + j % 2]


def side_kernel(came_ref, keep_ref, send_ref):
    side = (lax.axis_index("tp") // 2) % 2
    for out_ref, at in ((keep_ref, side), (send_ref, 1 - side)):
        piece = came_ref[0, at]
        for j in range(1, came_ref.shape[0]):
            piece += came_ref[j, at]
        out_ref[...] = piece


def add_kernel(mine_ref, came_ref, out_ref):
    out_ref[...] = mine_ref[...] + came_ref[...]


def relay_kernel(came_ref, out_ref):
    out_ref[...] = came_ref[...]


def spread_kernel(mine_ref, came_ref, copies_ref):
    copies_ref[...] = jnp.broadcast_to(mine_ref[...] + came_ref[...], copies_ref.shape)


def finish_kernel(
    sums_ref,
    params_ref,
    moment_ref,
    kept_ref,
    came_ref,
    params_out_ref,
    moment_out_ref,
    igrad_out_ref,
):
    rows = params_ref.shape[0]
    per_part = sums_ref.shape[1] // rows
    own = lax.axis_index("rep")
    for j in range(params_ref.shape[1] // block):
        cols = slice(j * block, (j + 1) * block)
        part, k = divmod(j, per_part)
        params_out_ref[:, cols] = (
            params_ref[:, cols] - param_step * sums_ref[part, k * rows : (k + 1) * rows]
        )
        moment_out_ref[:, cols] = (
            sums_ref[part, pl.ds(k * rows + own, 1), :] + moment_rest * moment_ref[:, cols]
        )
    igrad_out_ref[...] = (kept_ref[...] + came_ref[...]).astype(igrad_out_ref.dtype)


def swap(array, axis, bit):
    size = lax.axis_size(axis)
    return lax.ppermute(array, axis, [(i, i ^ bit) for i in range(size)])


def exchange(array, axis, groups):
    return lax.all_to_all(array, axis, 0, 0, axis_index_groups=groups, tiled=True)


def on_device(
    quant_codes, block_scales, outer_params, outer_moment, inputs, saved_pre, grad_out, weights
):
    groups = lax.axis_size("rep")
    _, rows, hidden = quant_codes.shape
    tokens, window = inputs.shape
    size = rows * hidden // (near * block)
    near_groups = [list(range(i, i + near)) for i in range(0, groups, near)]

    parts = pl.pallas_call(
        functools.partial(dequant_kernel, groups=groups),
        out_shape=jax.ShapeDtypeStruct((near, size, block), jnp.float32),
        name="dequant",
    )(quant_codes, jnp.transpose(block_scales, (0, 2, 1)), outer_moment)
    parts, inputs = lax.optimization_barrier((parts, inputs))
    parts = exchange(parts, "rep", near_groups)
    chunk = jnp.sum(parts, axis=0)

    tile = 1536
    shares = lax.axis_size("tp")
    piece = (window // shares, tokens)
    sent = jax.ShapeDtypeStruct((shares // 2, 2) + piece, jnp.float32)
    weight_grad, send = pl.pallas_call(
        backward_kernel,
        grid=(hidden // tile,),
        in_specs=[
            full((tokens, window)),
            pl.BlockSpec((tokens, tile), lambda i: (0, i)),
            pl.BlockSpec((tokens, tile), lambda i: (0, i)),
            pl.BlockSpec((1, window, tile), lambda i: (0, 0, i)),
        ],
        out_specs=[
            pl.BlockSpec((1, window, tile), lambda i: (0, 0, i)),
            full(sent.shape),
        ],
        out_shape=(jax.ShapeDtypeStruct((1, window, hidden), jnp.bfloat16), sent),
        scratch_shapes=[pltpu.VMEM((shares,) + piece, jnp.float32)],
        cost_estimate=pl.CostEstimate(
            flops=4 * tokens * window * hidden,
            bytes_accessed=4 * tokens * hidden + 4 * window * hidden,
            transcendentals=tokens * hidden,
        ),
        compiler_params=pltpu.CompilerParams(vmem_limit_bytes=60 << 20),
        name="backward",
    )(inputs, saved_pre, grad_out, weights)

    chunk, _ = lax.optimization_barrier((chunk, send))
    column_groups = [
        [i + side + core for i in range(0, shares, 4) for core in (0, 1)] for side in (0, 2)
    ]
    came = exchange(send, "tp", column_groups)
    part = jax.ShapeDtypeStruct(piece, jnp.float32)
    keep, send = pl.pallas_call(
        side_kernel, out_shape=(part, part), compiler_params=small, name="column_sum"
    )(came)
    places = [(i, j) for i in range(groups) for j in range(shares)]
    came = lax.ppermute(
        send,
        ("rep", "tp"),
        [(i * shares + j, (i ^ (near if j & 2 else 2 * near)) * shares + (j ^ 2)) for i, j in places],
    )
    moved = swap(chunk, "rep", near)
    chunk = pl.pallas_call(
        add_kernel,
        out_shape=jax.ShapeDtypeStruct(chunk.shape, jnp.float32),
        compiler_params=small,
        cost_estimate=pl.CostEstimate(flops=10**11, bytes_accessed=10**9, transcendentals=0),
        name="pair_sum",
    )(chunk, moved)
    moved = swap(chunk, "rep", 2 * near)
    copies = pl.pallas_call(
        spread_kernel,
        out_shape=jax.ShapeDtypeStruct((near, size, block), jnp.float32),
        compiler_params=small,
        name="spread",
    )(chunk, moved)
    came = pl.pallas_call(
        relay_kernel,
        out_shape=part,
        compiler_params=small,
        cost_estimate=pl.CostEstimate(flops=10**11, bytes_accessed=10**9, transcendentals=0),
        name="relay",
    )(came)
    came = lax.ppermute(
        came,
        ("rep", "tp"),
        [(i * shares + j, (i ^ (2 * near if j & 2 else near)) * shares + j) for i, j in places],
    )
    sums = exchange(copies, "rep", near_groups)
    new_params, new_moment, input_grad_t = pl.pallas_call(
        finish_kernel,
        out_shape=(
            jax.ShapeDtypeStruct(outer_params.shape, jnp.float32),
            jax.ShapeDtypeStruct(outer_moment.shape, jnp.float32),
            jax.ShapeDtypeStruct(piece, jnp.bfloat16),
        ),
        compiler_params=small,
        name="finish",
    )(sums, outer_params, outer_moment, keep, came)
    return (new_params, new_moment, weight_grad, input_grad_t)


def solution(mesh):
    in_specs = (
        P("rep", None, "tp"),
        P("rep", None, "tp"),
        P(None, "tp"),
        P("rep", "tp"),
        P("rep", None),
        P("rep", "tp"),
        P("rep", "tp"),
        P("rep", None, "tp"),
    )
    out_specs = (P(None, "tp"), P("rep", "tp"), P("rep", None, "tp"), P("tp", "rep"))
    return jax.shard_map(
        on_device, mesh=mesh, in_specs=in_specs, out_specs=out_specs, check_vma=False
    )
```

```python
import functools

import jax
import jax.numpy as jnp
from jax import lax
from jax.experimental import pallas as pl
from jax.experimental.pallas import tpu as pltpu
from jax.sharding import PartitionSpec as P

outer_rate = 0.7
outer_momentum = 0.9
slope_scale = 0.7978845608028654
carry = outer_momentum * outer_momentum / (1.0 + outer_momentum)
param_step = outer_rate * (1.0 + outer_momentum)
moment_rest = outer_momentum - carry
near = 8
block = 128
small = pltpu.CompilerParams(vmem_limit_bytes=4 << 20)


def full(shape):
    return pl.BlockSpec(shape, lambda *_: (0,) * len(shape))


def dequant_kernel(codes_ref, scales_ref, moment_ref, out_ref, *, groups):
    rows = codes_ref.shape[1]
    per_part = out_ref.shape[1] // rows
    own = lax.broadcasted_iota(jnp.int32, (rows, block), 0) == lax.axis_index("rep")
    scales = scales_ref[0].T * (1.0 / groups)
    for j in range(codes_ref.shape[2] // block):
        cols = slice(j * block, (j + 1) * block)
        grads = (codes_ref[0, :, cols].astype(jnp.float32) - 7.5) * scales[:, j : j + 1]
        kept = jnp.where(own, carry * moment_ref[:, cols], 0.0)
        part, k = divmod(j, per_part)
        out_ref[part, k * rows : (k + 1) * rows] = grads + kept


def backward_kernel(
    inputs_ref, pre_ref, grad_ref, weights_ref, wgrad_ref, send_ref, total
):
    step = pl.program_id(0)

    @pl.when(step == 0)
    def _():
        total[...] = jnp.zeros_like(total)

    v = pre_ref[...].astype(jnp.float32)
    u = v * v
    t = jnp.tanh(v * (slope_scale + (slope_scale * 0.044715) * u))
    slope = (0.5 + 0.5 * t) * (
        1.0 + (v * (slope_scale + (slope_scale * 0.134145) * u)) * (1.0 - t)
    )
    pre_grad = (grad_ref[...].astype(jnp.float32) * slope).astype(jnp.bfloat16)
    wgrad_ref[0] = lax.dot_general(
        inputs_ref[...], pre_grad, (((0,), (0,)), ((), ())), preferred_element_type=jnp.float32
    ).astype(jnp.bfloat16)
    total[...] += lax.dot_general(
        weights_ref[0], pre_grad, (((1,), (1,)), ((), ())), preferred_element_type=jnp.float32
    ).reshape(total.shape)

    @pl.when(step == pl.num_programs(0) - 1)
    def _():
        columns, sides = send_ref.shape[:2]
        for j in range(columns):
            for side in range(sides):
                send_ref[j, side] = total[(j // 2) * 4 + side * 2 + j % 2]


def side_kernel(came_ref, keep_ref, send_ref):
    side = (lax.axis_index("tp") // 2) % 2
    for out_ref, at in ((keep_ref, side), (send_ref, 1 - side)):
        piece = came_ref[0, at]
        for j in range(1, came_ref.shape[0]):
            piece += came_ref[j, at]
        out_ref[...] = piece


def add_kernel(mine_ref, came_ref, out_ref):
    out_ref[...] = mine_ref[...] + came_ref[...]


def relay_kernel(came_ref, out_ref):
    out_ref[...] = came_ref[...]


def spread_kernel(mine_ref, came_ref, copies_ref):
    copies_ref[...] = jnp.broadcast_to(mine_ref[...] + came_ref[...], copies_ref.shape)


def finish_kernel(
    sums_ref,
    params_ref,
    moment_ref,
    kept_ref,
    came_ref,
    params_out_ref,
    moment_out_ref,
    igrad_out_ref,
):
    rows = params_ref.shape[0]
    per_part = sums_ref.shape[1] // rows
    own = lax.axis_index("rep")
    for j in range(params_ref.shape[1] // block):
        cols = slice(j * block, (j + 1) * block)
        part, k = divmod(j, per_part)
        params_out_ref[:, cols] = (
            params_ref[:, cols] - param_step * sums_ref[part, k * rows : (k + 1) * rows]
        )
        moment_out_ref[:, cols] = (
            sums_ref[part, pl.ds(k * rows + own, 1), :] + moment_rest * moment_ref[:, cols]
        )
    igrad_out_ref[...] = (kept_ref[...] + came_ref[...]).astype(igrad_out_ref.dtype)


def swap(array, axis, bit):
    size = lax.axis_size(axis)
    return lax.ppermute(array, axis, [(i, i ^ bit) for i in range(size)])


def exchange(array, axis, groups):
    return lax.all_to_all(array, axis, 0, 0, axis_index_groups=groups, tiled=True)


def on_device(
    quant_codes, block_scales, outer_params, outer_moment, inputs, saved_pre, grad_out, weights
):
    groups = lax.axis_size("rep")
    _, rows, hidden = quant_codes.shape
    tokens, window = inputs.shape
    size = rows * hidden // (near * block)
    near_groups = [list(range(i, i + near)) for i in range(0, groups, near)]

    parts = pl.pallas_call(
        functools.partial(dequant_kernel, groups=groups),
        out_shape=jax.ShapeDtypeStruct((near, size, block), jnp.float32),
        name="dequant",
    )(quant_codes, jnp.transpose(block_scales, (0, 2, 1)), outer_moment)
    parts, inputs = lax.optimization_barrier((parts, inputs))
    parts = exchange(parts, "rep", near_groups)
    chunk = jnp.sum(parts, axis=0)

    tile = 1536
    shares = lax.axis_size("tp")
    piece = (window // shares, tokens)
    sent = jax.ShapeDtypeStruct((shares // 2, 2) + piece, jnp.float32)
    weight_grad, send = pl.pallas_call(
        backward_kernel,
        grid=(hidden // tile,),
        in_specs=[
            full((tokens, window)),
            pl.BlockSpec((tokens, tile), lambda i: (0, i)),
            pl.BlockSpec((tokens, tile), lambda i: (0, i)),
            pl.BlockSpec((1, window, tile), lambda i: (0, 0, i)),
        ],
        out_specs=[
            pl.BlockSpec((1, window, tile), lambda i: (0, 0, i)),
            full(sent.shape),
        ],
        out_shape=(jax.ShapeDtypeStruct((1, window, hidden), jnp.bfloat16), sent),
        scratch_shapes=[pltpu.VMEM((shares,) + piece, jnp.float32)],
        cost_estimate=pl.CostEstimate(
            flops=4 * tokens * window * hidden,
            bytes_accessed=4 * tokens * hidden + 4 * window * hidden,
            transcendentals=tokens * hidden,
        ),
        compiler_params=pltpu.CompilerParams(vmem_limit_bytes=60 << 20),
        name="backward",
    )(inputs, saved_pre, grad_out, weights)

    chunk, _ = lax.optimization_barrier((chunk, send))
    column_groups = [
        [i + side + core for i in range(0, shares, 4) for core in (0, 1)] for side in (0, 2)
    ]
    came = exchange(send, "tp", column_groups)
    part = jax.ShapeDtypeStruct(piece, jnp.float32)
    keep, send = pl.pallas_call(
        side_kernel, out_shape=(part, part), compiler_params=small, name="column_sum"
    )(came)
    places = [(i, j) for i in range(groups) for j in range(shares)]
    came = lax.ppermute(
        send,
        ("rep", "tp"),
        [(i * shares + j, (i ^ (near if j & 2 else 3 * near)) * shares + (j ^ 2)) for i, j in places],
    )
    moved = swap(chunk, "rep", near)
    chunk = pl.pallas_call(
        add_kernel,
        out_shape=jax.ShapeDtypeStruct(chunk.shape, jnp.float32),
        compiler_params=small,
        cost_estimate=pl.CostEstimate(flops=10**11, bytes_accessed=10**9, transcendentals=0),
        name="pair_sum",
    )(chunk, moved)
    moved = swap(chunk, "rep", 2 * near)
    copies = pl.pallas_call(
        spread_kernel,
        out_shape=jax.ShapeDtypeStruct((near, size, block), jnp.float32),
        compiler_params=small,
        name="spread",
    )(chunk, moved)
    came = pl.pallas_call(
        relay_kernel,
        out_shape=part,
        compiler_params=small,
        cost_estimate=pl.CostEstimate(flops=10**11, bytes_accessed=10**9, transcendentals=0),
        name="relay",
    )(came)
    came = lax.ppermute(
        came,
        ("rep", "tp"),
        [(i * shares + j, (i ^ (3 * near if j & 2 else near)) * shares + j) for i, j in places],
    )
    sums = exchange(copies, "rep", near_groups)
    new_params, new_moment, input_grad_t = pl.pallas_call(
        finish_kernel,
        out_shape=(
            jax.ShapeDtypeStruct(outer_params.shape, jnp.float32),
            jax.ShapeDtypeStruct(outer_moment.shape, jnp.float32),
            jax.ShapeDtypeStruct(piece, jnp.bfloat16),
        ),
        compiler_params=small,
        name="finish",
    )(sums, outer_params, outer_moment, keep, came)
    return (new_params, new_moment, weight_grad, input_grad_t)


def solution(mesh):
    in_specs = (
        P("rep", None, "tp"),
        P("rep", None, "tp"),
        P(None, "tp"),
        P("rep", "tp"),
        P("rep", None),
        P("rep", "tp"),
        P("rep", "tp"),
        P("rep", None, "tp"),
    )
    out_specs = (P(None, "tp"), P("rep", "tp"), P("rep", None, "tp"), P("tp", "rep"))
    return jax.shard_map(
        on_device, mesh=mesh, in_specs=in_specs, out_specs=out_specs, check_vma=False
    )
```

```python
import functools

import jax
import jax.numpy as jnp
from jax import lax
from jax.experimental import pallas as pl
from jax.experimental.pallas import tpu as pltpu
from jax.sharding import PartitionSpec as P

outer_rate = 0.7
outer_momentum = 0.9
slope_scale = 0.7978845608028654
carry = outer_momentum * outer_momentum / (1.0 + outer_momentum)
param_step = outer_rate * (1.0 + outer_momentum)
moment_rest = outer_momentum - carry
near = 8
block = 128
small = pltpu.CompilerParams(vmem_limit_bytes=4 << 20)


def full(shape):
    return pl.BlockSpec(shape, lambda *_: (0,) * len(shape))


def dequant_kernel(codes_ref, scales_ref, moment_ref, out_ref, *, groups):
    rows = codes_ref.shape[1]
    per_part = out_ref.shape[1] // rows
    own = lax.broadcasted_iota(jnp.int32, (rows, block), 0) == lax.axis_index("rep")
    scales = scales_ref[0].T * (1.0 / groups)
    for j in range(codes_ref.shape[2] // block):
        cols = slice(j * block, (j + 1) * block)
        grads = (codes_ref[0, :, cols].astype(jnp.float32) - 7.5) * scales[:, j : j + 1]
        kept = jnp.where(own, carry * moment_ref[:, cols], 0.0)
        part, k = divmod(j, per_part)
        out_ref[part, k * rows : (k + 1) * rows] = grads + kept


def backward_kernel(
    inputs_ref, pre_ref, grad_ref, weights_ref, wgrad_ref, send_ref, total
):
    step = pl.program_id(0)

    @pl.when(step == 0)
    def _():
        total[...] = jnp.zeros_like(total)

    v = pre_ref[...].astype(jnp.float32)
    u = v * v
    t = jnp.tanh(v * (slope_scale + (slope_scale * 0.044715) * u))
    slope = (0.5 + 0.5 * t) * (
        1.0 + (v * (slope_scale + (slope_scale * 0.134145) * u)) * (1.0 - t)
    )
    pre_grad = (grad_ref[...].astype(jnp.float32) * slope).astype(jnp.bfloat16)
    wgrad_ref[0] = lax.dot_general(
        inputs_ref[...], pre_grad, (((0,), (0,)), ((), ())), preferred_element_type=jnp.float32
    ).astype(jnp.bfloat16)
    total[...] += lax.dot_general(
        weights_ref[0], pre_grad, (((1,), (1,)), ((), ())), preferred_element_type=jnp.float32
    ).reshape(total.shape)

    @pl.when(step == pl.num_programs(0) - 1)
    def _():
        columns, sides = send_ref.shape[:2]
        for j in range(columns):
            for side in range(sides):
                send_ref[j, side] = total[(j // 2) * 4 + side * 2 + j % 2]


def side_kernel(came_ref, keep_ref, send_ref):
    side = (lax.axis_index("tp") // 2) % 2
    for out_ref, at in ((keep_ref, side), (send_ref, 1 - side)):
        piece = came_ref[0, at]
        for j in range(1, came_ref.shape[0]):
            piece += came_ref[j, at]
        out_ref[...] = piece


def add_kernel(mine_ref, came_ref, out_ref):
    out_ref[...] = mine_ref[...] + came_ref[...]


def relay_kernel(kept_ref, came_ref, sum_ref, out_ref):
    out_ref[...] = came_ref[...]
    upper = (lax.axis_index("tp") // 2) % 2
    sum_ref[...] = kept_ref[...] + jnp.where(upper == 0, came_ref[...], 0.0)


def spread_kernel(mine_ref, came_ref, copies_ref):
    copies_ref[...] = jnp.broadcast_to(mine_ref[...] + came_ref[...], copies_ref.shape)


def finish_kernel(
    sums_ref,
    params_ref,
    moment_ref,
    kept_ref,
    came_ref,
    params_out_ref,
    moment_out_ref,
    igrad_out_ref,
):
    rows = params_ref.shape[0]
    per_part = sums_ref.shape[1] // rows
    own = lax.axis_index("rep")
    for j in range(params_ref.shape[1] // block):
        cols = slice(j * block, (j + 1) * block)
        part, k = divmod(j, per_part)
        params_out_ref[:, cols] = (
            params_ref[:, cols] - param_step * sums_ref[part, k * rows : (k + 1) * rows]
        )
        moment_out_ref[:, cols] = (
            sums_ref[part, pl.ds(k * rows + own, 1), :] + moment_rest * moment_ref[:, cols]
        )
    igrad_out_ref[...] = (kept_ref[...] + came_ref[...]).astype(igrad_out_ref.dtype)


def swap(array, axis, bit):
    size = lax.axis_size(axis)
    return lax.ppermute(array, axis, [(i, i ^ bit) for i in range(size)])


def exchange(array, axis, groups):
    return lax.all_to_all(array, axis, 0, 0, axis_index_groups=groups, tiled=True)


def on_device(
    quant_codes, block_scales, outer_params, outer_moment, inputs, saved_pre, grad_out, weights
):
    groups = lax.axis_size("rep")
    _, rows, hidden = quant_codes.shape
    tokens, window = inputs.shape
    size = rows * hidden // (near * block)
    near_groups = [list(range(i, i + near)) for i in range(0, groups, near)]

    parts = pl.pallas_call(
        functools.partial(dequant_kernel, groups=groups),
        out_shape=jax.ShapeDtypeStruct((near, size, block), jnp.float32),
        name="dequant",
    )(quant_codes, jnp.transpose(block_scales, (0, 2, 1)), outer_moment)
    parts, inputs = lax.optimization_barrier((parts, inputs))
    parts = exchange(parts, "rep", near_groups)
    chunk = jnp.sum(parts, axis=0)

    tile = 1536
    shares = lax.axis_size("tp")
    piece = (window // shares, tokens)
    sent = jax.ShapeDtypeStruct((shares // 2, 2) + piece, jnp.float32)
    weight_grad, send = pl.pallas_call(
        backward_kernel,
        grid=(hidden // tile,),
        in_specs=[
            full((tokens, window)),
            pl.BlockSpec((tokens, tile), lambda i: (0, i)),
            pl.BlockSpec((tokens, tile), lambda i: (0, i)),
            pl.BlockSpec((1, window, tile), lambda i: (0, 0, i)),
        ],
        out_specs=[
            pl.BlockSpec((1, window, tile), lambda i: (0, 0, i)),
            full(sent.shape),
        ],
        out_shape=(jax.ShapeDtypeStruct((1, window, hidden), jnp.bfloat16), sent),
        scratch_shapes=[pltpu.VMEM((shares,) + piece, jnp.float32)],
        cost_estimate=pl.CostEstimate(
            flops=4 * tokens * window * hidden,
            bytes_accessed=4 * tokens * hidden + 4 * window * hidden,
            transcendentals=tokens * hidden,
        ),
        compiler_params=pltpu.CompilerParams(vmem_limit_bytes=60 << 20),
        name="backward",
    )(inputs, saved_pre, grad_out, weights)

    chunk, _ = lax.optimization_barrier((chunk, send))
    column_groups = [
        [i + side + core for i in range(0, shares, 4) for core in (0, 1)] for side in (0, 2)
    ]
    came = exchange(send, "tp", column_groups)
    part = jax.ShapeDtypeStruct(piece, jnp.float32)
    keep, send = pl.pallas_call(
        side_kernel, out_shape=(part, part), compiler_params=small, name="column_sum"
    )(came)
    places = [(i, j) for i in range(groups) for j in range(shares)]
    came = lax.ppermute(
        send,
        ("rep", "tp"),
        [(i * shares + j, (i if j & 2 else i ^ (3 * near)) * shares + (j ^ 2)) for i, j in places],
    )
    moved = swap(chunk, "rep", near)
    chunk = pl.pallas_call(
        add_kernel,
        out_shape=jax.ShapeDtypeStruct(chunk.shape, jnp.float32),
        compiler_params=small,
        cost_estimate=pl.CostEstimate(flops=10**11, bytes_accessed=10**9, transcendentals=0),
        name="pair_sum",
    )(chunk, moved)
    moved = swap(chunk, "rep", 2 * near)
    copies = pl.pallas_call(
        spread_kernel,
        out_shape=jax.ShapeDtypeStruct((near, size, block), jnp.float32),
        compiler_params=small,
        name="spread",
    )(chunk, moved)
    keep, came = pl.pallas_call(
        relay_kernel,
        out_shape=(part, part),
        compiler_params=small,
        cost_estimate=pl.CostEstimate(flops=10**11, bytes_accessed=10**9, transcendentals=0),
        name="relay",
    )(keep, came)
    came = lax.ppermute(
        came,
        ("rep", "tp"),
        [(i * shares + j, (i ^ (3 * near)) * shares + j) for i, j in places if j & 2],
    )
    sums = exchange(copies, "rep", near_groups)
    new_params, new_moment, input_grad_t = pl.pallas_call(
        finish_kernel,
        out_shape=(
            jax.ShapeDtypeStruct(outer_params.shape, jnp.float32),
            jax.ShapeDtypeStruct(outer_moment.shape, jnp.float32),
            jax.ShapeDtypeStruct(piece, jnp.bfloat16),
        ),
        compiler_params=small,
        name="finish",
    )(sums, outer_params, outer_moment, keep, came)
    return (new_params, new_moment, weight_grad, input_grad_t)


def solution(mesh):
    in_specs = (
        P("rep", None, "tp"),
        P("rep", None, "tp"),
        P(None, "tp"),
        P("rep", "tp"),
        P("rep", None),
        P("rep", "tp"),
        P("rep", "tp"),
        P("rep", None, "tp"),
    )
    out_specs = (P(None, "tp"), P("rep", "tp"), P("rep", None, "tp"), P("tp", "rep"))
    return jax.shard_map(
        on_device, mesh=mesh, in_specs=in_specs, out_specs=out_specs, check_vma=False
    )
```
